512 devices in a mesh: tp: 8 (over z), ad: 64 (over y, x, core).
Axes of the slice: x: 4, y: 8, z: 8, core: 2. Of those that a mesh axis runs over, the one named last changes fastest.
Arguments:
- tokens: bfloat16 [65536, 8192], P('ad', 'tp'), may hold values from -6 to 6
- value_weight: bfloat16 [8192, 1024], P(('tp', 'ad')), may hold values from -0.0625 to 0.0625
- adapter_down: bfloat16 [128, 8192, 128], P('ad', 'tp'), may hold values from -0.0625 to 0.0625
- adapter_up_panels: bfloat16 [128, 128, 1024], P('ad', None, 'tp'), may hold values from -0.5 to 0.5
- req_start: int32 [64], replicated, may hold values from 0 to 65280, as said below
- req_adapter: int32 [64], replicated, may hold values from 0 to 127
- adapter_home: int32 [128], replicated, may hold values from 0 to 127, each once
Outputs:
- adapted: bfloat16 [65536, 1024], P('ad', 'tp')
The draws below stay inside these ranges and needn't reach their ends.
Inputs may be any that keep to these rules, and one draw needn't show every extreme that they name: `req_start`: entries rise strictly, the first is 0 and each is a multiple of 256; the tokens of one index of ad meet at most 4 requests, and those of the first index meet exactly 4. Each storage row once; adapter a is stored on index adapter_home[a] // 2 of ad.
All inputs are finite; a program needn't handle non-finite values.
Results may differ from the reference program's by a relative error of at most 0.0085.
Values may be sent and summed in bfloat16 or wider, within the bound.
A program may use at most 64 MiB of HBM per device.

```python
import math
import jax
import jax.numpy as jnp
import numpy as np
from jax import lax

D = 8192
KV = 1024
R = 128
TOK_DEV = 1024
FMAX = 4
REQS = 64
ADAPTERS = 128
TOKENS = 65536


def draw_req_start(key, part):
    block_rows = TOK_DEV // FMAX
    block_count = TOKENS // block_rows
    shuffled = jax.random.permutation(key, block_count - FMAX - 1) + FMAX
    picked = jnp.sort(shuffled[:REQS - FMAX - 1])
    starts = jnp.concatenate([jnp.arange(FMAX, dtype=jnp.int32), picked.astype(jnp.int32), jnp.full((1,), block_count - 1, jnp.int32)])
    return (starts * block_rows).astype(jnp.int32)


def plant(array, stream_key, low, high):
    longest = array.shape.index(max(array.shape))
    spots = []
    for shift in (0, 1):
        where = [jax.random.randint(jax.random.fold_in(stream_key, axis), (), 0, length) for axis, length in enumerate(array.shape)]
        where[longest] = (where[longest] + shift) % array.shape[longest]
        spots.append(tuple(where))
    return array.at[spots[0]].set(low).at[spots[1]].set(high)


def shard_levels(key, dims, cuts, low, top_value):
    gain, own = 1.0, jax.random.fold_in(key, 6)
    for axis_at, shards_of in cuts:
        steps = jnp.exp(jax.random.uniform(jax.random.fold_in(own, axis_at), (shards_of,), jnp.float32, low / len(cuts), top_value / len(cuts)))
        gain = gain * jnp.repeat(steps, dims[axis_at] // shards_of).reshape([-1 if axis == axis_at else 1 for axis in range(len(dims))])
    return gain


def rank_table(count, lean):
    loads = [(1 << 20) // math.isqrt(grade ** lean) + 1 for grade in range(1, count + 1)]
    scale = 1 + sum(loads) // (1 << 30)
    return np.cumsum(np.array([max(1, weight // scale) for weight in loads]))


def ranked_ids(stream_key, shape, count, skew):
    grid = rank_table(count, skew)
    pick = jax.random.randint(jax.random.fold_in(stream_key, 1), shape, 0, int(grid[count - 1]))
    rank = jnp.searchsorted(jnp.asarray(grid, jnp.int32), pick, side="right")
    return jax.random.permutation(jax.random.fold_in(stream_key, 2), count)[rank].astype(jnp.int32)


def scatter_about(own_key, dims, scale, reach, shards=(), kind=jnp.bfloat16):
    result = jax.random.normal(own_key, dims, jnp.float32) * scale
    if len(shards) > 0:
        result = shard_levels(own_key, dims, shards, -0.22, 0.18) * result
    return jnp.clip(result, min=-reach, max=reach).astype(kind)


def setup_inputs(seed: int = 0) -> dict:
    streams_of = jax.random.split(jax.random.key(seed), 8)
    tokens = scatter_about(streams_of[0], (TOKENS, D), 1.0, 6.0, ((0, 64), (1, 8)))
    value_weight = scatter_about(streams_of[1], (D, KV), D ** -0.5, 0.0625, ((0, 512),))
    adapter_down = scatter_about(streams_of[2], (ADAPTERS, D, R), D ** -0.5, 0.0625, ((0, 64), (1, 8)))
    adapter_up_panels = scatter_about(streams_of[3], (ADAPTERS, R, KV), R ** -0.5, 0.5, ((0, 64), (2, 8)))
    req_start = draw_req_start(jax.random.fold_in(streams_of[7], 71), 0)
    req_adapter = plant(ranked_ids(streams_of[5], (REQS,), ADAPTERS, 2), jax.random.fold_in(streams_of[5], 3), 0, ADAPTERS - 1).astype(jnp.int32)
    adapter_home = jax.random.permutation(streams_of[6], ADAPTERS).astype(jnp.int32)
    return {"tokens": tokens, "value_weight": value_weight, "adapter_down": adapter_down, "adapter_up_panels": adapter_up_panels, "req_start": req_start, "req_adapter": req_adapter, "adapter_home": adapter_home}


adapter_scale = 2.0


def reference(tokens, value_weight, adapter_down, adapter_up_panels, req_start, req_adapter, adapter_home):
    block_rows = TOK_DEV // FMAX
    blocks = TOKENS // block_rows
    first_rows = jnp.arange(blocks, dtype=jnp.int32) * block_rows
    request = jnp.sum((req_start[None, :] <= first_rows[:, None]).astype(jnp.int32), axis=1) - 1
    adapter = req_adapter[request.astype(jnp.int32)]
    stored = adapter_home[adapter.astype(jnp.int32)].astype(jnp.int32)
    tok_blocks = tokens.reshape(blocks, block_rows, D)

    def one_block(block_args):
        row_block, storage_row_index = block_args
        base_value_output = jnp.dot(row_block, value_weight, preferred_element_type=jnp.float32)
        down_panel = adapter_down[storage_row_index]
        adapter_rank_rows = jnp.dot(row_block, down_panel, preferred_element_type=jnp.float32).astype(jnp.bfloat16)
        adapter_value_delta = jnp.dot(adapter_rank_rows, adapter_up_panels[storage_row_index], preferred_element_type=jnp.float32)
        return (base_value_output + adapter_scale * adapter_value_delta).astype(jnp.bfloat16)

    adapted = lax.map(one_block, (tok_blocks, stored))
    return adapted.reshape(TOKENS, KV)
```

```python
import functools

import jax
import jax.numpy as jnp
from jax import lax
from jax.experimental import pallas as pl
from jax.experimental.pallas import tpu as pltpu
from jax.sharding import PartitionSpec as P

BF = jnp.bfloat16
F32 = jnp.float32
MESH = pl.DeviceIdType.MESH

ROW = 8
NX = 4
NT = 8
NY = 8
BLK = 4
SPREAD = (1, 7, 2, 6, 3, 5, 4)
PIECES = (4, 3, 5, 2, 6, 1, 7, 0)
ADAPTER_SCALE = 2.0


def kernel(
    tok_h, vw_h, down_h, up_h, start_s, adap_s, home_s,
    out_ref,
    tok, wy, wb, dnrow, slab, dsel, drow, dfin,
    uprow, uperm, upslab, upsel, uprcv, upx, upg,
    zs, zr, part, rsend, rrecv, rfull, ids,
    loc_sem, w1s, w1r, w2s, w2r, w3s, w3r,
    a1s, a1r, u1s, u1r, b1s, b1r, v1s, v1r,
    a2s, a2r, u2s, u2r, b2s, b2r, v2s, v2r,
    zss, zrs, rss, rsr, rgs, rgr,
):
    t = lax.axis_index("tp")
    a = lax.axis_index("ad")
    y = a // ROW
    q = a % ROW
    x = q // 2
    c = q % 2

    def ydev(d):
        return (t, ((y + d) % NY) * ROW + q)

    def rdev(e):
        return (t, y * ROW + (q + e) % ROW)

    def xdev(f):
        return (t, y * ROW + ((x + f) % NX) * 2 + c)

    def tdev(k):
        return ((t + k) % NT, a)

    sib = (t, y * ROW + x * 2 + (1 - c))

    bar = pltpu.get_barrier_semaphore()
    for d in range(1, NY):
        pl.semaphore_signal(bar, inc=1, device_id=ydev(d), device_id_type=MESH)
    for e in range(1, ROW):
        pl.semaphore_signal(bar, inc=1, device_id=rdev(e), device_id_type=MESH)
    for k in range(1, NT):
        pl.semaphore_signal(bar, inc=1, device_id=tdev(k), device_id_type=MESH)
    pl.semaphore_wait(bar, 21)

    sent = []

    def remote(src, dst, s, r, dev):
        cp = pltpu.make_async_remote_copy(
            src_ref=src, dst_ref=dst, send_sem=s, recv_sem=r, device_id=dev, device_id_type=MESH
        )
        cp.start()
        sent.append(cp)
        return cp

    def local(src, dst, i):
        cp = pltpu.make_async_copy(src, dst, loc_sem.at[i])
        cp.start()
        return cp

    a1 = [
        remote(down_h.at[:, (q + e) % ROW], dnrow.at[pl.ds(2 * q, 2)], a1s.at[e], a1r.at[e], rdev(e))
        for e in SPREAD
    ]
    cd = local(down_h.at[:, q], dnrow.at[pl.ds(2 * q, 2)], 1)
    w1 = [remote(vw_h, wy.at[y], w1s.at[d], w1r.at[d], ydev(d)) for d in SPREAD]
    cw = local(vw_h, wy.at[y], 0)
    u1 = [
        remote(up_h.at[:, (q + e) % ROW], uprow.at[pl.ds(2 * q, 2)], u1s.at[e], u1r.at[e], rdev(e))
        for e in SPREAD
    ]
    cu = local(up_h.at[:, q], uprow.at[pl.ds(2 * q, 2)], 2)
    ct = local(tok_h, tok, 3)

    cd.wait()
    for cp in a1:
        cp.wait_recv()
    b1 = [
        remote(dnrow.at[:, (y + d) % NY], slab.at[pl.ds(16 * y, 16)], b1s.at[d], b1r.at[d], ydev(d))
        for d in SPREAD
    ]
    cs = local(dnrow.at[:, y], slab.at[pl.ds(16 * y, 16)], 4)
    def cols(o):
        return pl.ds(pl.multiple_of(((t + o) % NT) * 128, 128), 128)

    cw.wait()
    for cp in w1:
        cp.wait_recv()
    w2 = []
    for p, o in enumerate(PIECES):
        w2.append([
            remote(
                wy.at[:, :, cols(o)], wb[p].at[c, x],
                w2s.at[p, f], w2r.at[p, f], xdev(f),
            )
            for f in (1, 3, 2)
        ])
        wb[p][c, x] = wy[:, :, cols(o)]

    cu.wait()
    for cp in u1:
        cp.wait_recv()
    ro = lax.broadcasted_iota(jnp.int32, (256, 256), 0)
    ri = lax.broadcasted_iota(jnp.int32, (256, 256), 1)
    src = ((ro // 2) % 16) * 16 + (ro // 32) * 2 + ro % 2
    uperm[...] = jnp.dot(
        (src == ri).astype(BF), uprow[...].reshape(256, 128), preferred_element_type=F32
    ).astype(BF).reshape(NY, 32, 128)
    v1 = [
        remote(uperm.at[(y + d) % NY], upslab.at[y], v1s.at[d], v1r.at[d], ydev(d)) for d in SPREAD
    ]
    upslab[y] = uperm[y]

    def block_id(b, req):
        nxt = jnp.minimum(req + 1, start_s.shape[0] - 1)
        hit = jnp.where(start_s[nxt] <= b * 256, 1, 0)
        req = jnp.where(nxt > req, req + hit, req)
        ids[b] = home_s[adap_s[req]]
        return req

    lax.fori_loop(0, NY * ROW * BLK, block_id, jnp.int32(0))

    w3 = {}

    def w_forward(p):
        for cp in w2[p]:
            cp.wait_recv()
        w3[p] = remote(wb[p].at[c], wb[p].at[c], w3s.at[p], w3r.at[p], sib)

    def partial(p):
        w3[p].wait_recv()
        w = jnp.concatenate(
            [wb[p][k, j, i] for i in range(NY) for j in range(NX) for k in range(2)], axis=0
        )

        def rows(g, _):
            r = pl.ds(pl.multiple_of(g * 256, 256), 256)
            part[p, r, :] = jnp.dot(tok[r, :], w, preferred_element_type=F32)
            return 0

        lax.fori_loop(0, BLK, rows, 0)

    zc = {}

    def zsend(i, k, g):
        way = (1, -1)[i]
        zc[i, k, g] = remote(
            zs[i][k].at[g], zr[i][k].at[g], zss.at[i, k, g], zrs.at[i, k, g], tdev(way)
        )

    def zstep(i, k, p):
        for g in ((0, 1, 2, 3), (2, 3, 0, 1))[i]:
            if k == 0 and g // 2 != i:
                continue
            v = part[p, pl.ds(g * 256, 256), :]
            if (i, k - 1, g) in zc:
                zc[i, k - 1, g].wait_recv()
                v = v + zr[i][k - 1][g].astype(F32)
            zs[i][k][g] = v.astype(BF)
            zsend(i, k, g)

    ct.wait()
    w_forward(0)
    w_forward(1)
    partial(0)
    zstep(0, 0, 0)
    zstep(1, 0, 0)
    w_forward(2)
    partial(1)
    w_forward(3)
    partial(2)
    zstep(0, 1, 1)
    zstep(1, 1, 2)
    w_forward(4)
    partial(3)
    w_forward(5)
    partial(4)
    w_forward(6)
    w_forward(7)

    cs.wait()
    for cp in b1:
        cp.wait_recv()

    def pick(i, _):
        for j in range(ROW):
            for s in range(BLK):
                dsel[s][i, j] = slab[ids[i * (ROW * BLK) + (j * BLK + s)]]
        return 0

    lax.fori_loop(0, NY, pick, 0)
    b2 = []
    for s in range(BLK):
        b2.append([
            remote(
                dsel[s].at[(y + d) % NY], drow[s].at[y], b2s.at[s, d], b2r.at[s, d], ydev(d)
            )
            for d in SPREAD
        ])
        drow[s][y] = dsel[s][y]

    zstep(0, 2, 3)
    zstep(1, 2, 4)
    partial(5)
    partial(6)
    partial(7)
    zstep(0, 3, 5)
    zstep(1, 3, 6)

    for cp in v1:
        cp.wait_recv()
    half = lax.broadcasted_iota(jnp.int32, (16, 256), 0) // 2
    odd = lax.broadcasted_iota(jnp.int32, (16, 256), 0) % 2
    col = lax.broadcasted_iota(jnp.int32, (16, 256), 1)
    upall = upslab[...].reshape(256, 128)

    def pick_up(n, _):
        want = odd
        for k in range(8):
            want = jnp.where(half == k, want + 2 * ids[n * 8 + k], want)
        hot = (want == col).astype(BF)
        upsel[n] = jnp.dot(hot, upall, preferred_element_type=F32).astype(BF)
        return 0

    lax.fori_loop(0, 32, pick_up, 0)
    v2 = [
        remote(
            upsel.at[pl.ds(4 * ((y + d) % NY), 4)], uprcv.at[pl.ds(4 * y, 4)],
            v2s.at[d], v2r.at[d], ydev(d),
        )
        for d in SPREAD
    ]
    uprcv[pl.ds(4 * y, 4)] = upsel[pl.ds(4 * y, 4)]

    a2 = {}

    def row_send(s):
        for cp in b2[s]:
            cp.wait_recv()
        a2[s] = [
            remote(
                drow[s].at[:, (q + e) % ROW], dfin[s].at[q], a2s.at[s, e], a2r.at[s, e], rdev(e)
            )
            for e in SPREAD
        ]
        dfin[s][q] = drow[s][:, q]

    rs = {}

    def rank(s):
        for cp in a2[s]:
            cp.wait_recv()
        v = jnp.dot(
            tok[pl.ds(s * 256, 256), :], dfin[s][...].reshape(1024, 128), preferred_element_type=F32
        )
        rsend[s][...] = v.astype(BF).reshape(NT, 32, 128)
        rs[s] = [
            remote(rsend[s].at[(t + k) % NT], rrecv[s].at[t], rss.at[s, k], rsr.at[s, k], tdev(k))
            for k in SPREAD
        ]
        rrecv[s][t] = rsend[s][t]

    rg = {}

    def rank_sum(s):
        for cp in rs[s]:
            cp.wait_recv()
        v = jnp.sum(rrecv[s][...].astype(F32), axis=0)
        rfull[s][t] = v.astype(BF)
        rg[s] = [
            remote(rfull[s].at[t], rfull[s].at[t], rgs.at[s, k], rgr.at[s, k], tdev(k))
            for k in SPREAD
        ]

    row_send(0)
    row_send(1)
    rank(0)
    row_send(2)
    rank(1)
    rank_sum(0)
    row_send(3)

    for cp in v2:
        cp.wait_recv()
    ro = lax.broadcasted_iota(jnp.int32, (512, 512), 0)
    ri = lax.broadcasted_iota(jnp.int32, (512, 512), 1)
    src = ((ro // 2) % 8) * 64 + (ro // 64) * 8 + ((ro // 16) % 4) * 2 + ro % 2
    upx[...] = jnp.dot(
        (src == ri).astype(BF), uprcv[...].reshape(512, 128), preferred_element_type=F32
    ).astype(BF).reshape(ROW, BLK, 16, 128)
    u2 = [
        remote(upx.at[(q + e) % ROW], upg.at[q], u2s.at[e], u2r.at[e], rdev(e)) for e in SPREAD
    ]
    upg[q] = upx[q]

    rank(2)
    rank_sum(1)
    rank(3)
    rank_sum(2)
    rank_sum(3)

    for g in range(BLK):
        zc[0, 3, g].wait_recv()
        zc[1, 3, g].wait_recv()
        r = pl.ds(g * 256, 256)
        part[7, r, :] = part[7, r, :] + zr[0][3][g].astype(F32) + zr[1][3][g].astype(F32)
    for cp in u2:
        cp.wait_recv()
    for s in range(BLK):
        for cp in rg[s]:
            cp.wait_recv()
        delta = jnp.dot(
            rfull[s][...].reshape(256, 128), upg[:, s].reshape(128, 128), preferred_element_type=F32
        )
        r = pl.ds(s * 256, 256)
        out_ref[r, :] = (part[7, r, :] + ADAPTER_SCALE * delta).astype(BF)
    for cp in sent:
        cp.wait_send()


def body(tokens, value_weight, down, up, req_start, req_adapter, adapter_home):
    vm = pltpu.VMEM
    sem = pltpu.SemaphoreType.DMA
    any_ = pl.BlockSpec(memory_space=pl.ANY)
    smem = pl.BlockSpec(memory_space=pltpu.SMEM)
    return pl.pallas_call(
        kernel,
        out_shape=jax.ShapeDtypeStruct((1024, 128), BF),
        in_specs=[any_] * 4 + [smem] * 3,
        out_specs=pl.BlockSpec(memory_space=pltpu.VMEM),
        scratch_shapes=[
            vm((1024, 1024), BF),
            vm((NY, 16, 1024), BF),
            [vm((2, NX, NY, 16, 128), BF)] * NT,
            vm((16, NY, 16, 128), BF),
            vm((128, 16, 128), BF),
            [vm((NY, ROW, 16, 128), BF)] * BLK,
            [vm((NY, ROW, 16, 128), BF)] * BLK,
            [vm((ROW, NY, 16, 128), BF)] * BLK,
            vm((16, 16, 128), BF),
            vm((NY, 32, 128), BF),
            vm((NY, 32, 128), BF),
            vm((32, 16, 128), BF),
            vm((32, 16, 128), BF),
            vm((ROW, BLK, 16, 128), BF),
            vm((ROW, BLK, 16, 128), BF),
            [[vm((BLK, 256, 128), BF)] * 4] * 2,
            [[vm((BLK, 256, 128), BF)] * 4] * 2,
            vm((8, 1024, 128), F32),
            [vm((NT, 32, 128), BF)] * BLK,
            [vm((NT, 32, 128), BF)] * BLK,
            [vm((NT, 32, 128), BF)] * BLK,
            pltpu.SMEM((NY * ROW * BLK,), jnp.int32),
            sem((5,)),
            sem((8,)), sem((8,)), sem((8, 4)), sem((8, 4)), sem((8,)), sem((8,)),
            sem((8,)), sem((8,)), sem((8,)), sem((8,)), sem((8,)), sem((8,)), sem((8,)), sem((8,)),
            sem((4, 8)), sem((4, 8)), sem((8,)), sem((8,)), sem((4, 8)), sem((4, 8)), sem((8,)), sem((8,)),
            sem((2, 4, 4)), sem((2, 4, 4)),
            sem((4, 8)), sem((4, 8)), sem((4, 8)), sem((4, 8)),
        ],
        compiler_params=pltpu.CompilerParams(
            collective_id=0, has_side_effects=True, vmem_limit_bytes=60 * 1024 * 1024
        ),
    )(
        tokens, value_weight,
        down.reshape(2, ROW, NY, 16, 128), up.reshape(2, ROW, 16, 128),
        req_start, req_adapter, adapter_home,
    )


def solution(mesh):
    return jax.shard_map(
        body,
        mesh=mesh,
        in_specs=(
            P("ad", "tp"),
            P(("tp", "ad"), None),
            P("ad", "tp", None),
            P("ad", None, "tp"),
            P(),
            P(),
            P(),
        ),
        out_specs=P("ad", "tp"),
        check_vma=False,
    )
```

```python
import functools

import jax
import jax.numpy as jnp
from jax import lax
from jax.experimental import pallas as pl
from jax.experimental.pallas import tpu as pltpu
from jax.sharding import PartitionSpec as P

BF = jnp.bfloat16
F32 = jnp.float32
MESH = pl.DeviceIdType.MESH

ROW = 8
NX = 4
NT = 8
NY = 8
BLK = 4
SPREAD = (4, 3, 5, 2, 6, 1, 7)
PIECES = (4, 3, 5, 2, 6, 1, 7, 0)
ADAPTER_SCALE = 2.0


def kernel(
    tok_h, vw_h, down_h, up_h, start_s, adap_s, home_s,
    out_ref,
    tok, wy, wb, dnrow, slab, dsel, drow, dfin,
    uprow, uperm, upslab, upsel, uprcv, upx, upg,
    zs, zr, part, rsend, rrecv, rfull, order1, order2, ids,
    loc_sem, w1s, w1r, w2s, w2r, w3s, w3r,
    a1s, a1r, u1s, u1r, b1s, b1r, v1s, v1r,
    a2s, a2r, u2s, u2r, b2s, b2r, v2s, v2r,
    zss, zrs, rss, rsr, rgs, rgr,
):
    t = lax.axis_index("tp")
    a = lax.axis_index("ad")
    y = a // ROW
    q = a % ROW
    x = q // 2
    c = q % 2

    def ydev(d):
        return (t, ((y + d) % NY) * ROW + q)

    def rdev(e):
        return (t, y * ROW + (q + e) % ROW)

    def xdev(f):
        return (t, y * ROW + ((x + f) % NX) * 2 + c)

    def tdev(k):
        return ((t + k) % NT, a)

    sib = (t, y * ROW + x * 2 + (1 - c))

    bar = pltpu.get_barrier_semaphore()
    for d in range(1, NY):
        pl.semaphore_signal(bar, inc=1, device_id=ydev(d), device_id_type=MESH)
    for e in range(1, ROW):
        pl.semaphore_signal(bar, inc=1, device_id=rdev(e), device_id_type=MESH)
    for k in range(1, NT):
        pl.semaphore_signal(bar, inc=1, device_id=tdev(k), device_id_type=MESH)
    ro = lax.broadcasted_iota(jnp.int32, (256, 256), 0)
    ri = lax.broadcasted_iota(jnp.int32, (256, 256), 1)
    src = ((ro // 2) % 16) * 16 + (ro // 32) * 2 + ro % 2
    order1[...] = (src == ri).astype(BF)
    ro = lax.broadcasted_iota(jnp.int32, (512, 512), 0)
    ri = lax.broadcasted_iota(jnp.int32, (512, 512), 1)
    src = ((ro // 2) % 8) * 64 + (ro // 64) * 8 + ((ro // 16) % 4) * 2 + ro % 2
    order2[...] = (src == ri).astype(BF)

    def block_id(b, req):
        nxt = jnp.minimum(req + 1, start_s.shape[0] - 1)
        hit = jnp.where(start_s[nxt] <= b * 256, 1, 0)
        req = jnp.where(nxt > req, req + hit, req)
        ids[b] = home_s[adap_s[req]]
        return req

    lax.fori_loop(0, NY * ROW * BLK, block_id, jnp.int32(0))

    pl.semaphore_wait(bar, 21)

    sent = []

    def remote(src, dst, s, r, dev):
        cp = pltpu.make_async_remote_copy(
            src_ref=src, dst_ref=dst, send_sem=s, recv_sem=r, device_id=dev, device_id_type=MESH
        )
        cp.start()
        sent.append(cp)
        return cp

    def local(src, dst, i):
        cp = pltpu.make_async_copy(src, dst, loc_sem.at[i])
        cp.start()
        return cp

    a1 = [
        remote(down_h.at[:, (q + e) % ROW], dnrow.at[pl.ds(2 * q, 2)], a1s.at[e], a1r.at[e], rdev(e))
        for e in SPREAD
    ]
    cd = local(down_h.at[:, q], dnrow.at[pl.ds(2 * q, 2)], 1)
    w1 = [remote(vw_h, wy.at[y], w1s.at[d], w1r.at[d], ydev(d)) for d in SPREAD]
    cw = local(vw_h, wy.at[y], 0)
    u1 = [
        remote(up_h.at[:, (q + e) % ROW], uprow.at[pl.ds(2 * q, 2)], u1s.at[e], u1r.at[e], rdev(e))
        for e in SPREAD
    ]
    cu = local(up_h.at[:, q], uprow.at[pl.ds(2 * q, 2)], 2)
    ct = local(tok_h, tok, 3)

    cd.wait()
    for cp in a1:
        cp.wait_recv()
    b1 = [
        remote(dnrow.at[:, (y + d) % NY], slab.at[pl.ds(16 * y, 16)], b1s.at[d], b1r.at[d], ydev(d))
        for d in SPREAD
    ]
    cs = local(dnrow.at[:, y], slab.at[pl.ds(16 * y, 16)], 4)
    def cols(o):
        return pl.ds(pl.multiple_of(((t + o) % NT) * 128, 128), 128)

    cw.wait()
    for cp in w1:
        cp.wait_recv()
    w2 = []
    for p, o in enumerate(PIECES):
        w2.append([
            remote(
                wy.at[:, :, cols(o)], wb[p].at[c, x],
                w2s.at[p, f], w2r.at[p, f], xdev(f),
            )
            for f in (1, 3, 2)
        ])
        wb[p][c, x] = wy[:, :, cols(o)]

    cu.wait()
    for cp in u1:
        cp.wait_recv()
    uperm[...] = jnp.dot(
        order1[...], uprow[...].reshape(256, 128), preferred_element_type=F32
    ).astype(BF).reshape(NY, 32, 128)
    v1 = [
        remote(uperm.at[(y + d) % NY], upslab.at[y], v1s.at[d], v1r.at[d], ydev(d)) for d in SPREAD
    ]
    upslab[y] = uperm[y]

    w3 = {}

    def w_forward(p):
        for cp in w2[p]:
            cp.wait_recv()
        w3[p] = remote(wb[p].at[c], wb[p].at[c], w3s.at[p], w3r.at[p], sib)

    def partial(p):
        w3[p].wait_recv()
        w = jnp.concatenate(
            [wb[p][k, j, i] for i in range(NY) for j in range(NX) for k in range(2)], axis=0
        )

        def rows(g, _):
            r = pl.ds(pl.multiple_of(g * 256, 256), 256)
            part[p, r, :] = jnp.dot(tok[r, :], w, preferred_element_type=F32)
            return 0

        lax.fori_loop(0, BLK, rows, 0)

    zc = {}

    def zsend(i, k, g):
        way = (1, -1)[i]
        zc[i, k, g] = remote(
            zs[i][k].at[g], zr[i][k].at[g], zss.at[i, k, g], zrs.at[i, k, g], tdev(way)
        )

    def zstep(i, k, p):
        for g in ((0, 1, 2, 3), (2, 3, 0, 1))[i]:
            if k == 0 and g // 2 != i:
                continue
            v = part[p, pl.ds(g * 256, 256), :]
            if (i, k - 1, g) in zc:
                zc[i, k - 1, g].wait_recv()
                v = v + zr[i][k - 1][g].astype(F32)
            zs[i][k][g] = v.astype(BF)
            zsend(i, k, g)

    ct.wait()
    w_forward(0)
    w_forward(1)
    partial(0)
    zstep(0, 0, 0)
    zstep(1, 0, 0)
    w_forward(2)
    partial(1)
    w_forward(3)
    partial(2)
    zstep(0, 1, 1)
    zstep(1, 1, 2)
    w_forward(4)
    partial(3)
    w_forward(5)
    partial(4)
    w_forward(6)
    w_forward(7)

    cs.wait()
    for cp in b1:
        cp.wait_recv()

    b2 = []
    for s in range(BLK):
        def pick(i, _):
            for j in range(ROW):
                dsel[s][i, j] = slab[ids[i * (ROW * BLK) + (j * BLK + s)]]
            return 0

        lax.fori_loop(0, NY, pick, 0)
        b2.append([
            remote(
                dsel[s].at[(y + d) % NY], drow[s].at[y], b2s.at[s, d], b2r.at[s, d], ydev(d)
            )
            for d in SPREAD
        ])
        drow[s][y] = dsel[s][y]

    zstep(0, 2, 3)
    zstep(1, 2, 4)
    partial(5)
    partial(6)
    partial(7)
    zstep(0, 3, 5)
    zstep(1, 3, 6)

    for cp in v1:
        cp.wait_recv()
    half = lax.broadcasted_iota(jnp.int32, (16, 256), 0) // 2
    odd = lax.broadcasted_iota(jnp.int32, (16, 256), 0) % 2
    col = lax.broadcasted_iota(jnp.int32, (16, 256), 1)
    upall = upslab[...].reshape(256, 128)

    def pick_up(n, _):
        want = odd
        for k in range(8):
            want = jnp.where(half == k, want + 2 * ids[n * 8 + k], want)
        hot = (want == col).astype(BF)
        upsel[n] = jnp.dot(hot, upall, preferred_element_type=F32).astype(BF)
        return 0

    lax.fori_loop(0, 32, pick_up, 0)
    v2 = [
        remote(
            upsel.at[pl.ds(4 * ((y + d) % NY), 4)], uprcv.at[pl.ds(4 * y, 4)],
            v2s.at[d], v2r.at[d], ydev(d),
        )
        for d in SPREAD
    ]
    uprcv[pl.ds(4 * y, 4)] = upsel[pl.ds(4 * y, 4)]

    a2 = {}

    def row_send(s):
        for cp in b2[s]:
            cp.wait_recv()
        a2[s] = [
            remote(
                drow[s].at[:, (q + e) % ROW], dfin[s].at[q], a2s.at[s, e], a2r.at[s, e], rdev(e)
            )
            for e in SPREAD
        ]
        dfin[s][q] = drow[s][:, q]

    rs = {}

    def rank(s):
        for cp in a2[s]:
            cp.wait_recv()
        v = jnp.dot(
            tok[pl.ds(s * 256, 256), :], dfin[s][...].reshape(1024, 128), preferred_element_type=F32
        )
        rsend[s][...] = v.astype(BF).reshape(NT, 32, 128)
        rs[s] = [
            remote(rsend[s].at[(t + k) % NT], rrecv[s].at[t], rss.at[s, k], rsr.at[s, k], tdev(k))
            for k in SPREAD
        ]
        rrecv[s][t] = rsend[s][t]

    rg = {}

    def rank_sum(s):
        for cp in rs[s]:
            cp.wait_recv()
        v = jnp.sum(rrecv[s][...].astype(F32), axis=0)
        rfull[s][t] = v.astype(BF)
        rg[s] = [
            remote(rfull[s].at[t], rfull[s].at[t], rgs.at[s, k], rgr.at[s, k], tdev(k))
            for k in SPREAD
        ]

    def out(s):
        for cp in rg[s]:
            cp.wait_recv()
        delta = jnp.dot(
            rfull[s][...].reshape(256, 128), upg[:, s].reshape(128, 128), preferred_element_type=F32
        )
        r = pl.ds(s * 256, 256)
        out_ref[r, :] = (part[7, r, :] + ADAPTER_SCALE * delta).astype(BF)

    row_send(0)
    row_send(1)
    rank(0)
    row_send(2)
    rank(1)
    rank_sum(0)
    for g in range(BLK):
        zc[0, 3, g].wait_recv()
        zc[1, 3, g].wait_recv()
        r = pl.ds(g * 256, 256)
        part[7, r, :] = part[7, r, :] + zr[0][3][g].astype(F32) + zr[1][3][g].astype(F32)
    row_send(3)
    rank_sum(1)
    rank(2)
    for cp in v2:
        cp.wait_recv()
    upx[...] = jnp.dot(
        order2[...], uprcv[...].reshape(512, 128), preferred_element_type=F32
    ).astype(BF).reshape(ROW, BLK, 16, 128)
    u2 = [
        remote(upx.at[(q + e) % ROW], upg.at[q], u2s.at[e], u2r.at[e], rdev(e)) for e in SPREAD
    ]
    upg[q] = upx[q]

    rank(3)
    rank_sum(2)
    for cp in u2:
        cp.wait_recv()
    out(0)
    out(1)
    rank_sum(3)
    out(2)
    out(3)
    for cp in sent:
        cp.wait_send()


def body(tokens, value_weight, down, up, req_start, req_adapter, adapter_home):
    vm = pltpu.VMEM
    sem = pltpu.SemaphoreType.DMA
    any_ = pl.BlockSpec(memory_space=pl.ANY)
    smem = pl.BlockSpec(memory_space=pltpu.SMEM)
    return pl.pallas_call(
        kernel,
        out_shape=jax.ShapeDtypeStruct((1024, 128), BF),
        in_specs=[any_] * 4 + [smem] * 3,
        out_specs=pl.BlockSpec(memory_space=pltpu.VMEM),
        scratch_shapes=[
            vm((1024, 1024), BF),
            vm((NY, 16, 1024), BF),
            [vm((2, NX, NY, 16, 128), BF)] * NT,
            vm((16, NY, 16, 128), BF),
            vm((128, 16, 128), BF),
            [vm((NY, ROW, 16, 128), BF)] * BLK,
            [vm((NY, ROW, 16, 128), BF)] * BLK,
            [vm((ROW, NY, 16, 128), BF)] * BLK,
            vm((16, 16, 128), BF),
            vm((NY, 32, 128), BF),
            vm((NY, 32, 128), BF),
            vm((32, 16, 128), BF),
            vm((32, 16, 128), BF),
            vm((ROW, BLK, 16, 128), BF),
            vm((ROW, BLK, 16, 128), BF),
            [[vm((BLK, 256, 128), BF)] * 4] * 2,
            [[vm((BLK, 256, 128), BF)] * 4] * 2,
            vm((8, 1024, 128), F32),
            [vm((NT, 32, 128), BF)] * BLK,
            [vm((NT, 32, 128), BF)] * BLK,
            [vm((NT, 32, 128), BF)] * BLK,
            vm((256, 256), BF),
            vm((512, 512), BF),
            pltpu.SMEM((NY * ROW * BLK,), jnp.int32),
            sem((5,)),
            sem((8,)), sem((8,)), sem((8, 4)), sem((8, 4)), sem((8,)), sem((8,)),
            sem((8,)), sem((8,)), sem((8,)), sem((8,)), sem((8,)), sem((8,)), sem((8,)), sem((8,)),
            sem((4, 8)), sem((4, 8)), sem((8,)), sem((8,)), sem((4, 8)), sem((4, 8)), sem((8,)), sem((8,)),
            sem((2, 4, 4)), sem((2, 4, 4)),
            sem((4, 8)), sem((4, 8)), sem((4, 8)), sem((4, 8)),
        ],
        compiler_params=pltpu.CompilerParams(
            collective_id=0, has_side_effects=True, vmem_limit_bytes=60 * 1024 * 1024
        ),
    )(
        tokens, value_weight,
        down.reshape(2, ROW, NY, 16, 128), up.reshape(2, ROW, 16, 128),
        req_start, req_adapter, adapter_home,
    )


def solution(mesh):
    return jax.shard_map(
        body,
        mesh=mesh,
        in_specs=(
            P("ad", "tp"),
            P(("tp", "ad"), None),
            P("ad", "tp", None),
            P("ad", None, "tp"),
            P(),
            P(),
            P(),
        ),
        out_specs=P("ad", "tp"),
        check_vma=False,
    )
```

```python
import functools

import jax
import jax.numpy as jnp
from jax import lax
from jax.experimental import pallas as pl
from jax.experimental.pallas import tpu as pltpu
from jax.sharding import PartitionSpec as P

BF = jnp.bfloat16
F32 = jnp.float32
MESH = pl.DeviceIdType.MESH

ROW = 8
NX = 4
NT = 8
NY = 8
BLK = 4
SPREAD = (4, 3, 5, 2, 6, 1, 7)
PIECES = (4, 3, 5, 2, 6, 1, 7, 0)
ADAPTER_SCALE = 2.0


def kernel(
    tok_h, vw_h, down_h, up_h, start_s, adap_s, home_s,
    out_ref,
    tok, wy, wb, dnrow, slab, dsel, drow, dfin,
    uprow, uperm, upslab, upsel, uprcv, upx, upg,
    zs, zr, part, rsend, rrecv, rfull, order1, order2, ids,
    loc_sem, w1s, w1r, w2s, w2r, w3s, w3r,
    a1s, a1r, u1s, u1r, b1s, b1r, v1s, v1r,
    a2s, a2r, u2s, u2r, b2s, b2r, v2s, v2r,
    zss, zrs, rss, rsr, rgs, rgr,
):
    t = lax.axis_index("tp")
    a = lax.axis_index("ad")
    y = a // ROW
    q = a % ROW
    x = q // 2
    c = q % 2

    def ydev(d):
        return (t, ((y + d) % NY) * ROW + q)

    def rdev(e):
        return (t, y * ROW + (q + e) % ROW)

    def xdev(f):
        return (t, y * ROW + ((x + f) % NX) * 2 + c)

    def tdev(k):
        return ((t + k) % NT, a)

    sib = (t, y * ROW + x * 2 + (1 - c))

    bar = pltpu.get_barrier_semaphore()
    for d in range(1, NY):
        pl.semaphore_signal(bar, inc=1, device_id=ydev(d), device_id_type=MESH)
    for e in range(1, ROW):
        pl.semaphore_signal(bar, inc=1, device_id=rdev(e), device_id_type=MESH)
    for k in range(1, NT):
        pl.semaphore_signal(bar, inc=1, device_id=tdev(k), device_id_type=MESH)
    ro = lax.broadcasted_iota(jnp.int32, (256, 256), 0)
    ri = lax.broadcasted_iota(jnp.int32, (256, 256), 1)
    src = ((ro // 2) % 16) * 16 + (ro // 32) * 2 + ro % 2
    order1[...] = (src == ri).astype(BF)
    ro = lax.broadcasted_iota(jnp.int32, (512, 512), 0)
    ri = lax.broadcasted_iota(jnp.int32, (512, 512), 1)
    src = ((ro // 2) % 8) * 64 + (ro // 64) * 8 + ((ro // 16) % 4) * 2 + ro % 2
    order2[...] = (src == ri).astype(BF)

    def block_id(b, req):
        nxt = jnp.minimum(req + 1, start_s.shape[0] - 1)
        hit = jnp.where(start_s[nxt] <= b * 256, 1, 0)
        req = jnp.where(nxt > req, req + hit, req)
        ids[b] = home_s[adap_s[req]]
        return req

    lax.fori_loop(0, NY * ROW * BLK, block_id, jnp.int32(0))

    pl.semaphore_wait(bar, 21)

    sent = []

    def remote(src, dst, s, r, dev):
        cp = pltpu.make_async_remote_copy(
            src_ref=src, dst_ref=dst, send_sem=s, recv_sem=r, device_id=dev, device_id_type=MESH
        )
        cp.start()
        sent.append(cp)
        return cp

    def local(src, dst, i):
        cp = pltpu.make_async_copy(src, dst, loc_sem.at[i])
        cp.start()
        return cp

    a1 = [
        remote(down_h.at[:, (q + e) % ROW], dnrow.at[pl.ds(2 * q, 2)], a1s.at[e], a1r.at[e], rdev(e))
        for e in SPREAD
    ]
    cd = local(down_h.at[:, q], dnrow.at[pl.ds(2 * q, 2)], 1)
    w1 = [remote(vw_h, wy.at[y], w1s.at[d], w1r.at[d], ydev(d)) for d in SPREAD]
    cw = local(vw_h, wy.at[y], 0)
    u1 = [
        remote(up_h.at[:, (q + e) % ROW], uprow.at[pl.ds(2 * q, 2)], u1s.at[e], u1r.at[e], rdev(e))
        for e in SPREAD
    ]
    cu = local(up_h.at[:, q], uprow.at[pl.ds(2 * q, 2)], 2)
    ct = local(tok_h, tok, 3)

    cd.wait()
    for cp in a1:
        cp.wait_recv()
    b1 = [
        remote(dnrow.at[:, (y + d) % NY], slab.at[pl.ds(16 * y, 16)], b1s.at[d], b1r.at[d], ydev(d))
        for d in SPREAD
    ]
    cs = local(dnrow.at[:, y], slab.at[pl.ds(16 * y, 16)], 4)
    def cols(o):
        return pl.ds(pl.multiple_of(((t + o) % NT) * 128, 128), 128)

    cw.wait()
    for cp in w1:
        cp.wait_recv()
    w2 = []
    for p, o in enumerate(PIECES):
        w2.append([
            remote(
                wy.at[:, :, cols(o)], wb[p].at[c, x],
                w2s.at[p, f], w2r.at[p, f], xdev(f),
            )
            for f in (1, 3, 2)
        ])
        wb[p][c, x] = wy[:, :, cols(o)]

    cu.wait()
    for cp in u1:
        cp.wait_recv()
    uperm[...] = jnp.dot(
        order1[...], uprow[...].reshape(256, 128), preferred_element_type=F32
    ).astype(BF).reshape(NY, 32, 128)
    v1 = [
        remote(uperm.at[(y + d) % NY], upslab.at[y], v1s.at[d], v1r.at[d], ydev(d)) for d in SPREAD
    ]
    upslab[y] = uperm[y]

    w3 = {}

    def w_forward(p):
        for cp in w2[p]:
            cp.wait_recv()
        w3[p] = remote(wb[p].at[c], wb[p].at[c], w3s.at[p], w3r.at[p], sib)

    def partial(p):
        w3[p].wait_recv()
        w = jnp.concatenate(
            [wb[p][k, j, i] for i in range(NY) for j in range(NX) for k in range(2)], axis=0
        )

        def rows(g, _):
            r = pl.ds(pl.multiple_of(g * 256, 256), 256)
            part[p, r, :] = jnp.dot(tok[r, :], w, preferred_element_type=F32)
            return 0

        lax.fori_loop(0, BLK, rows, 0)

    zc = {}

    def zsend(i, k, g):
        way = (1, -1)[i]
        zc[i, k, g] = remote(
            zs[i][k].at[g], zr[i][k].at[g], zss.at[i, k, g], zrs.at[i, k, g], tdev(way)
        )

    def zstep(i, k, p):
        for g in ((0, 1), (1, 0))[i]:
            if k == 0 and g != i:
                continue
            v = part[p, pl.ds(g * 512, 512), :]
            if (i, k - 1, g) in zc:
                zc[i, k - 1, g].wait_recv()
                v = v + zr[i][k - 1][g].astype(F32)
            zs[i][k][g] = v.astype(BF)
            zsend(i, k, g)

    ct.wait()
    w_forward(0)
    w_forward(1)
    partial(0)
    zstep(0, 0, 0)
    zstep(1, 0, 0)
    w_forward(2)
    partial(1)
    w_forward(3)
    partial(2)
    zstep(0, 1, 1)
    zstep(1, 1, 2)
    w_forward(4)
    partial(3)
    w_forward(5)
    partial(4)
    w_forward(6)
    w_forward(7)

    cs.wait()
    for cp in b1:
        cp.wait_recv()

    b2 = []
    for s in range(BLK):
        def pick(i, _):
            for j in range(ROW):
                dsel[s][i, j] = slab[ids[i * (ROW * BLK) + (j * BLK + s)]]
            return 0

        lax.fori_loop(0, NY, pick, 0)
        b2.append([
            remote(
                dsel[s].at[(y + d) % NY], drow[s].at[y], b2s.at[s, d], b2r.at[s, d], ydev(d)
            )
            for d in SPREAD
        ])
        drow[s][y] = dsel[s][y]

    zstep(0, 2, 3)
    zstep(1, 2, 4)
    partial(5)
    partial(6)
    partial(7)
    zstep(0, 3, 5)
    zstep(1, 3, 6)

    for cp in v1:
        cp.wait_recv()
    half = lax.broadcasted_iota(jnp.int32, (16, 256), 0) // 2
    odd = lax.broadcasted_iota(jnp.int32, (16, 256), 0) % 2
    col = lax.broadcasted_iota(jnp.int32, (16, 256), 1)
    upall = upslab[...].reshape(256, 128)

    def pick_up(n, _):
        want = odd
        for k in range(8):
            want = jnp.where(half == k, want + 2 * ids[n * 8 + k], want)
        hot = (want == col).astype(BF)
        upsel[n] = jnp.dot(hot, upall, preferred_element_type=F32).astype(BF)
        return 0

    lax.fori_loop(0, 32, pick_up, 0)
    v2 = [
        remote(
            upsel.at[pl.ds(4 * ((y + d) % NY), 4)], uprcv.at[pl.ds(4 * y, 4)],
            v2s.at[d], v2r.at[d], ydev(d),
        )
        for d in SPREAD
    ]
    uprcv[pl.ds(4 * y, 4)] = upsel[pl.ds(4 * y, 4)]

    a2 = {}

    def row_send(s):
        for cp in b2[s]:
            cp.wait_recv()
        a2[s] = [
            remote(
                drow[s].at[:, (q + e) % ROW], dfin[s].at[q], a2s.at[s, e], a2r.at[s, e], rdev(e)
            )
            for e in SPREAD
        ]
        dfin[s][q] = drow[s][:, q]

    rs = {}

    def rank(s):
        for cp in a2[s]:
            cp.wait_recv()
        v = jnp.dot(
            tok[pl.ds(s * 256, 256), :], dfin[s][...].reshape(1024, 128), preferred_element_type=F32
        )
        rsend[s][...] = v.astype(BF).reshape(NT, 32, 128)
        rs[s] = [
            remote(rsend[s].at[(t + k) % NT], rrecv[s].at[t], rss.at[s, k], rsr.at[s, k], tdev(k))
            for k in SPREAD
        ]
        rrecv[s][t] = rsend[s][t]

    rg = {}

    def rank_sum(s):
        for cp in rs[s]:
            cp.wait_recv()
        v = jnp.sum(rrecv[s][...].astype(F32), axis=0)
        rfull[s][t] = v.astype(BF)
        rg[s] = [
            remote(rfull[s].at[t], rfull[s].at[t], rgs.at[s, k], rgr.at[s, k], tdev(k))
            for k in SPREAD
        ]

    def out(s):
        for cp in rg[s]:
            cp.wait_recv()
        delta = jnp.dot(
            rfull[s][...].reshape(256, 128), upg[:, s].reshape(128, 128), preferred_element_type=F32
        )
        r = pl.ds(s * 256, 256)
        out_ref[r, :] = (part[7, r, :] + ADAPTER_SCALE * delta).astype(BF)

    row_send(0)
    row_send(1)
    rank(0)
    row_send(2)
    rank(1)
    rank_sum(0)
    for g in range(2):
        zc[0, 3, g].wait_recv()
        zc[1, 3, g].wait_recv()
        r = pl.ds(g * 512, 512)
        part[7, r, :] = part[7, r, :] + zr[0][3][g].astype(F32) + zr[1][3][g].astype(F32)
    row_send(3)
    rank_sum(1)
    rank(2)
    for cp in v2:
        cp.wait_recv()
    upx[...] = jnp.dot(
        order2[...], uprcv[...].reshape(512, 128), preferred_element_type=F32
    ).astype(BF).reshape(ROW, BLK, 16, 128)
    u2 = [
        remote(upx.at[(q + e) % ROW], upg.at[q], u2s.at[e], u2r.at[e], rdev(e)) for e in SPREAD
    ]
    upg[q] = upx[q]

    rank(3)
    rank_sum(2)
    for cp in u2:
        cp.wait_recv()
    out(0)
    out(1)
    rank_sum(3)
    out(2)
    out(3)
    for cp in sent:
        cp.wait_send()


def body(tokens, value_weight, down, up, req_start, req_adapter, adapter_home):
    vm = pltpu.VMEM
    sem = pltpu.SemaphoreType.DMA
    any_ = pl.BlockSpec(memory_space=pl.ANY)
    smem = pl.BlockSpec(memory_space=pltpu.SMEM)
    return pl.pallas_call(
        kernel,
        out_shape=jax.ShapeDtypeStruct((1024, 128), BF),
        in_specs=[any_] * 4 + [smem] * 3,
        out_specs=pl.BlockSpec(memory_space=pltpu.VMEM),
        scratch_shapes=[
            vm((1024, 1024), BF),
            vm((NY, 16, 1024), BF),
            [vm((2, NX, NY, 16, 128), BF)] * NT,
            vm((16, NY, 16, 128), BF),
            vm((128, 16, 128), BF),
            [vm((NY, ROW, 16, 128), BF)] * BLK,
            [vm((NY, ROW, 16, 128), BF)] * BLK,
            [vm((ROW, NY, 16, 128), BF)] * BLK,
            vm((16, 16, 128), BF),
            vm((NY, 32, 128), BF),
            vm((NY, 32, 128), BF),
            vm((32, 16, 128), BF),
            vm((32, 16, 128), BF),
            vm((ROW, BLK, 16, 128), BF),
            vm((ROW, BLK, 16, 128), BF),
            [[vm((2, 512, 128), BF)] * 4] * 2,
            [[vm((2, 512, 128), BF)] * 4] * 2,
            vm((8, 1024, 128), F32),
            [vm((NT, 32, 128), BF)] * BLK,
            [vm((NT, 32, 128), BF)] * BLK,
            [vm((NT, 32, 128), BF)] * BLK,
            vm((256, 256), BF),
            vm((512, 512), BF),
            pltpu.SMEM((NY * ROW * BLK,), jnp.int32),
            sem((5,)),
            sem((8,)), sem((8,)), sem((8, 4)), sem((8, 4)), sem((8,)), sem((8,)),
            sem((8,)), sem((8,)), sem((8,)), sem((8,)), sem((8,)), sem((8,)), sem((8,)), sem((8,)),
            sem((4, 8)), sem((4, 8)), sem((8,)), sem((8,)), sem((4, 8)), sem((4, 8)), sem((8,)), sem((8,)),
            sem((2, 4, 2)), sem((2, 4, 2)),
            sem((4, 8)), sem((4, 8)), sem((4, 8)), sem((4, 8)),
        ],
        compiler_params=pltpu.CompilerParams(
            collective_id=0, has_side_effects=True, vmem_limit_bytes=60 * 1024 * 1024
        ),
    )(
        tokens, value_weight,
        down.reshape(2, ROW, NY, 16, 128), up.reshape(2, ROW, 16, 128),
        req_start, req_adapter, adapter_home,
    )


def solution(mesh):
    return jax.shard_map(
        body,
        mesh=mesh,
        in_specs=(
            P("ad", "tp"),
            P(("tp", "ad"), None),
            P("ad", "tp", None),
            P("ad", None, "tp"),
            P(),
            P(),
            P(),
        ),
        out_specs=P("ad", "tp"),
        check_vma=False,
    )
```
